512 devices in a mesh: pair: 128 (over x_hi, y, z), row: 4 (over x_lo, core).
Axes of the slice: x: 4 (x_hi: 2, x_lo: 2; x = x_hi * 2 + x_lo), y: 8, z: 8, core: 2. Of those that a mesh axis runs over, the one named last changes fastest.
Arguments:
- statistic: bfloat16 [16384, 16384], P('row', 'pair'), may hold values from -1 to 12, as said below
- initial_basis: bfloat16 [16384, 16384], P('row', 'pair'), may hold values from -6 to 6
- moving_slot: int32 [4, 128], P(None, 'pair'), may hold values from 0 to 1
Outputs:
- eigvectors: float32 [16384, 16384], P('row', 'pair')
- spectrum: float32 [16384], P('pair')
- off_ratio: float32 [4], replicated
The draws below stay inside these ranges and needn't reach their ends.
Inputs may be any that keep to these rules, and one draw needn't show every extreme that they name: `statistic`: symmetric and positive definite. `moving_slot`: which of a pair's two blocks moves on.
All inputs are finite; a program needn't handle non-finite values.
Results may differ from the reference program's by a relative error of at most 0.0003.
Values sent between devices are 32-bit elements; how exact they have to be, the bound alone decides.
No kernel may reach another device: no remote copies, remote signals or barrier semaphores. Data moves between devices by JAX's collectives and lax.ppermute only.
A program may use at most 64 MiB of HBM per device.

```python
import math
import jax
import jax.numpy as jnp
from jax import lax

BLK = 64
ROUNDS = 4
INNER = 2
PAIRS = 128
M = 16384


def draw_statistic(key, part):
    noise_key = jax.random.fold_in(key, 11)
    diag_key = jax.random.fold_in(key, 12)
    noise = jnp.clip(jax.random.normal(noise_key, (M, M), jnp.float32), -4.0, 4.0)
    symmetric = (noise + noise.T) * (0.65 / math.sqrt(2.0 * M))
    spread = jax.random.uniform(diag_key, (M,), jnp.float32)
    diagonal = 2.0 * jnp.exp(spread * math.log(2.5))
    rising = 1.0 + 0.5 * jnp.arange(M, dtype=jnp.float32) / (M - 1)
    base = symmetric + jnp.eye(M, dtype=jnp.float32) * diagonal[None, :]
    return (rising[:, None] * rising[None, :] * base).astype(jnp.bfloat16)


def place_ends(entries, own_key, least, high):
    place = [jax.random.randint(jax.random.fold_in(own_key, axis), (), 0, length) for axis, length in enumerate(entries.shape)]
    main_axis = entries.shape.index(max(entries.shape))
    beside = place[:main_axis] + [(place[main_axis] + 1) % entries.shape[main_axis]] + place[main_axis + 1:]
    return entries.at[tuple(place)].set(least).at[tuple(beside)].set(high)


def steps_of(stream_key, extent, split, least, top_value):
    factor_of, own = 1.0, jax.random.fold_in(stream_key, 6)
    for dim, shards_of in split:
        draws = jnp.exp(jax.random.uniform(jax.random.fold_in(own, dim), (shards_of,), jnp.float32, least / len(split), top_value / len(split)))
        factor_of = factor_of * jnp.repeat(draws, extent[dim] // shards_of).reshape([-1 if axis == dim else 1 for axis in range(len(extent))])
    return factor_of


def bell_draw(own_key, dims, scale, most, cuts=(), held_as=jnp.bfloat16):
    result = jax.random.normal(own_key, dims, jnp.float32) * scale
    if len(cuts) > 0:
        result = steps_of(own_key, dims, cuts, -0.22, 0.18) * result
    return jnp.clip(result, min=-most, max=most).astype(held_as)


def setup_inputs(seed: int = 0) -> dict:
    key_list = jax.random.split(jax.random.key(seed), 4)
    return {
        "statistic": draw_statistic(jax.random.fold_in(key_list[3], 71), 0),
        "initial_basis": bell_draw(key_list[1], (M, M), 1.0, 6.0, ((0, 4), (1, 128))),
        "moving_slot": place_ends(jax.random.randint(key_list[2], (ROUNDS, PAIRS), 0, 2), jax.random.fold_in(key_list[2], 1), 0, 1).astype(jnp.int32),
    }


HIGH = lax.Precision.HIGHEST

def orthonormal(block):
    square = jnp.dot(block.T.astype(jnp.float32), block.astype(jnp.float32), precision=HIGH, preferred_element_type=jnp.float32)
    lower = jnp.linalg.cholesky(square)
    return jax.scipy.linalg.solve_triangular(lower, block.T, lower=True).T

def rotation(gram):
    basis = orthonormal(gram)
    for turn in range(INNER - 1):
        basis = orthonormal(jnp.dot(gram.astype(jnp.float32), basis.astype(jnp.float32), precision=HIGH, preferred_element_type=jnp.float32))
    return basis

def pair_round(pieces):
    factor, vectors = pieces
    gram = jnp.dot(factor.T.astype(jnp.float32), factor.astype(jnp.float32), precision=HIGH, preferred_element_type=jnp.float32)
    mask = jnp.eye(gram.shape[0], dtype=bool)
    squares = gram * gram
    off_part = jnp.sum(jnp.where(mask, jnp.float32(0.0), squares))
    diag_part = jnp.sum(jnp.where(mask, squares, jnp.float32(0.0)))
    basis = rotation(gram)
    new_factor = jnp.dot(factor.astype(jnp.float32), basis.astype(jnp.float32), precision=HIGH, preferred_element_type=jnp.float32)
    new_vectors = jnp.dot(vectors.astype(jnp.float32), basis.astype(jnp.float32), precision=HIGH, preferred_element_type=jnp.float32)
    return (new_factor, new_vectors, off_part, diag_part)

def move_blocks(blocks, slot):
    first = blocks[:, :, :BLK]
    second = blocks[:, :, BLK:]
    leaving = jnp.where(slot == 0, first, second)
    staying = jnp.where(slot == 0, second, first)
    arrived = jnp.roll(leaving, 1, axis=0)
    return jnp.where(slot == 0, jnp.concatenate([arrived, staying], axis=2), jnp.concatenate([staying, arrived], axis=2))

def reference(statistic, initial_basis, moving_slot):
    order = statistic.shape[0]
    width = 2 * BLK
    factor = statistic.astype(jnp.float32).reshape(order, PAIRS, width).transpose(1, 0, 2)
    vectors = initial_basis.astype(jnp.float32).reshape(order, PAIRS, width).transpose(1, 0, 2)
    ratios = []
    for step in range(ROUNDS):
        factor, vectors, off_part, diag_part = lax.map(pair_round, (factor, vectors))
        ratios.append(jnp.sqrt(jnp.sum(off_part) / jnp.sum(diag_part)))
        slot = moving_slot[step][:, None, None]
        factor = move_blocks(factor, slot)
        vectors = move_blocks(vectors, slot)
    spectrum = jnp.sqrt(lax.optimization_barrier(jnp.sum(factor * factor, axis=1))).reshape(order)
    eigvectors = vectors.transpose(1, 0, 2).reshape(order, order)
    return (eigvectors, spectrum, jnp.stack(ratios))
```

```python
import jax
import jax.numpy as jnp
from jax import lax
from jax.experimental import pallas as pl
from jax.experimental.pallas import tpu as pltpu
from jax.sharding import Mesh
from jax.sharding import PartitionSpec as P

ROUNDS = 4
PAIR = ("xh", "y", "z")
ROW = ("xl", "core")
SUB, WIDTH = 8, 128
TILES = WIDTH // SUB
HALF = WIDTH // 2

HIGHEST = lax.Precision.HIGHEST
HIGH = lax.Precision.HIGH


def spread(value):
    return jnp.broadcast_to(value, (SUB, WIDTH))


def tiles_of(matrix):
    return [matrix[SUB * t : SUB * (t + 1), :] for t in range(TILES)]


def eliminate(square, beside):
    square = tiles_of(square)
    beside = None if beside is None else tiles_of(beside)
    sub = lax.broadcasted_iota(jnp.int32, (SUB, WIDTH), 0)
    lane = lax.broadcasted_iota(jnp.int32, (SUB, WIDTH), 1)
    upper, solved = [], []
    for k in range(TILES):
        left = TILES - k
        cols = [[spread(square[t][:, SUB * k + m : SUB * k + m + 1]) for t in range(k, TILES)] for m in range(SUB)]
        pivots = None
        for j in range(SUB):
            pivot = spread(cols[j][0][j : j + 1, :])
            pivots = pivot if pivots is None else jnp.where(sub >= j, pivot, pivots)
            inverse = 1.0 / pivot
            coef = [c * inverse for c in cols[j]]
            coef[0] = jnp.where(sub > j, coef[0], 0.0)
            for m in range(j + 1, SUB):
                row = spread(cols[m][0][j : j + 1, :])
                for i in range(left):
                    cols[m][i] = cols[m][i] - coef[i] * row
            row = spread(square[k][j : j + 1, :])
            aside = None if beside is None else spread(beside[k][j : j + 1, :])
            for i in range(left):
                if i == 0 and j == SUB - 1:
                    continue
                square[k + i] = square[k + i] - coef[i] * row
                if beside is not None:
                    beside[k + i] = beside[k + i] - coef[i] * aside
        scale = lax.rsqrt(pivots)
        upper.append(jnp.where(lane >= sub + SUB * k, square[k] * scale, 0.0))
        if beside is not None:
            solved.append(beside[k] * scale)
    return jnp.concatenate(upper, axis=0), (jnp.concatenate(solved, axis=0) if solved else None)


def small(left, right, dims):
    return lax.dot_general(left, right, (dims, ((), ())), precision=HIGHEST, preferred_element_type=jnp.float32)


def rotation_kernel(parts_ref, basis_ref, sums_ref, norms_ref):
    gram = (parts_ref[0] + parts_ref[1]) + (parts_ref[2] + parts_ref[3])
    row = lax.broadcasted_iota(jnp.int32, gram.shape, 0)
    col = lax.broadcasted_iota(jnp.int32, gram.shape, 1)
    squares = gram * gram
    off = jnp.sum(jnp.where(row == col, 0.0, squares), axis=0, keepdims=True)
    diag = jnp.sum(jnp.where(row == col, squares, 0.0), axis=0, keepdims=True)
    sums_ref[...] = jnp.concatenate([off, diag], axis=0)
    upper, _ = eliminate(small(gram, gram, ((0,), (0,))), None)
    _, rows = eliminate(small(upper, upper, ((1,), (1,))), upper)
    basis = rows.T
    basis_ref[...] = basis
    norms_ref[...] = jnp.sum(basis * small(gram, basis, ((1,), (0,))), axis=0, keepdims=True)


def rotation(parts):
    return pl.pallas_call(
        rotation_kernel,
        out_shape=(
            jax.ShapeDtypeStruct((WIDTH, WIDTH), jnp.float32),
            jax.ShapeDtypeStruct((2, WIDTH), jnp.float32),
            jax.ShapeDtypeStruct((1, WIDTH), jnp.float32),
        ),
        name="rotation",
    )(parts)


def from_behind(value, steps=1):
    count = lax.axis_size(PAIR)
    return lax.ppermute(value, PAIR, [(source, (source + steps) % count) for source in range(count)])


def product(left, right):
    return jnp.dot(left, right, precision=HIGH, preferred_element_type=jnp.float32)


def inner(block):
    return lax.dot_general(
        block, block, (((0,), (0,)), ((), ())), precision=HIGHEST, preferred_element_type=jnp.float32
    )


def move(block, first):
    tall = block.shape[0] // 2
    leaving = jnp.where(first, block[:, :HALF], block[:, HALF:])
    staying = jnp.where(first, block[:, HALF:], block[:, :HALF])
    come = from_behind(jnp.concatenate([leaving[:tall], leaving[tall:]], axis=1))
    come = jnp.concatenate([come[:, :HALF], come[:, HALF:]], axis=0)
    return jnp.where(
        first, jnp.concatenate([come, staying], axis=1), jnp.concatenate([staying, come], axis=1)
    )


def on_device(statistic, initial_basis, moving_slot):
    factor = statistic.astype(jnp.float32)
    vectors = initial_basis.astype(jnp.float32)
    sums = []
    for step in range(ROUNDS):
        first = moving_slot[step, 0] == 0
        if step == 0:
            part = lax.dot_general(
                statistic, statistic, (((0,), (0,)), ((), ())), preferred_element_type=jnp.float32
            )
        else:
            part = inner(factor)
        basis, both, norms = rotation(lax.all_gather(part, ROW))
        sums.append(both)
        if step + 1 < ROUNDS:
            factor = move(product(factor, basis), first)
        vectors = move(product(vectors, basis), first)
    leaving = jnp.where(first, norms[:, :HALF], norms[:, HALF:])
    staying = jnp.where(first, norms[:, HALF:], norms[:, :HALF])
    come = from_behind(leaving)
    norms = jnp.where(
        first, jnp.concatenate([come, staying], axis=1), jnp.concatenate([staying, come], axis=1)
    )
    spectrum = jnp.sqrt(norms[0])
    total = jnp.concatenate(sums, axis=0)
    for axis in ("xh", "y", "z"):
        total = lax.psum(total, axis)
    total = jnp.sum(total.reshape(ROUNDS, 2, WIDTH), axis=2)
    return vectors, spectrum, jnp.sqrt(total[:, 0] / total[:, 1])


def solution(mesh):
    grid = Mesh(mesh.devices.reshape(2, 8, 8, 2, 2), PAIR + ROW)
    return jax.shard_map(
        on_device,
        mesh=grid,
        in_specs=(P(ROW, PAIR), P(ROW, PAIR), P(None, PAIR)),
        out_specs=(P(ROW, PAIR), P(PAIR), P()),
        check_vma=False,
    )
```

```python
import jax
import jax.numpy as jnp
from jax import lax
from jax.experimental import pallas as pl
from jax.experimental.pallas import tpu as pltpu
from jax.sharding import Mesh
from jax.sharding import PartitionSpec as P

ROUNDS = 4
PAIR = ("xh", "y", "z")
ROW = ("xl", "core")
SUB, WIDTH = 8, 128
TILES = WIDTH // SUB
HALF = WIDTH // 2
F32, BF16 = jnp.float32, jnp.bfloat16
HIGHEST = lax.Precision.HIGHEST
SMALL = jax.ShapeDtypeStruct((WIDTH, WIDTH), F32)
SMEM = pl.BlockSpec(memory_space=pltpu.SMEM)


def spread(value):
    return jnp.broadcast_to(value, (SUB, WIDTH))


def tiles_of(matrix):
    return [matrix[SUB * t : SUB * (t + 1), :] for t in range(TILES)]


def eliminate(square, beside):
    square = tiles_of(square)
    beside = None if beside is None else tiles_of(beside)
    sub = lax.broadcasted_iota(jnp.int32, (SUB, WIDTH), 0)
    lane = lax.broadcasted_iota(jnp.int32, (SUB, WIDTH), 1)
    upper, solved = [], []
    for k in range(TILES):
        left = TILES - k
        cols = [[spread(square[t][:, SUB * k + m : SUB * k + m + 1]) for t in range(k, TILES)] for m in range(SUB)]
        pivots = None
        for j in range(SUB):
            pivot = spread(cols[j][0][j : j + 1, :])
            pivots = pivot if pivots is None else jnp.where(sub >= j, pivot, pivots)
            inverse = 1.0 / pivot
            coef = [c * inverse for c in cols[j]]
            coef[0] = jnp.where(sub > j, coef[0], 0.0)
            for m in range(j + 1, SUB):
                row = spread(cols[m][0][j : j + 1, :])
                for i in range(left):
                    cols[m][i] = cols[m][i] - coef[i] * row
            row = spread(square[k][j : j + 1, :])
            aside = None if beside is None else spread(beside[k][j : j + 1, :])
            for i in range(left):
                if i == 0 and j == SUB - 1:
                    continue
                square[k + i] = square[k + i] - coef[i] * row
                if beside is not None:
                    beside[k + i] = beside[k + i] - coef[i] * aside
        scale = lax.rsqrt(pivots)
        upper.append(jnp.where(lane >= sub + SUB * k, square[k] * scale, 0.0))
        if beside is not None:
            solved.append(beside[k] * scale)
    return jnp.concatenate(upper, axis=0), (jnp.concatenate(solved, axis=0) if solved else None)


def small(left, right, dims=((1,), (0,))):
    return lax.dot_general(left, right, (dims, ((), ())), precision=HIGHEST, preferred_element_type=F32)


def lanes_over(value):
    return pltpu.roll(value, HALF, 1)


def rows_over(value):
    return jnp.concatenate([value[HALF:], value[:HALF]], axis=0)


def places():
    row = lax.broadcasted_iota(jnp.int32, (WIDTH, WIDTH), 0)
    col = lax.broadcasted_iota(jnp.int32, (WIDTH, WIDTH), 1)
    return row, col


def add_up(gram, sums_ref):
    row, col = places()
    squares = gram * gram
    off = jnp.sum(jnp.where(row == col, 0.0, squares), axis=0, keepdims=True)
    diag = jnp.sum(jnp.where(row == col, squares, 0.0), axis=0, keepdims=True)
    sums_ref[...] = jnp.concatenate([off, diag], axis=0)


def rotate(gram, own_slot, slot):
    placed = gram
    if own_slot is not None:
        placed = jnp.where(own_slot == 0, gram, rows_over(lanes_over(gram)))
    upper, _ = eliminate(small(placed, placed, ((0,), (0,))), None)
    _, rows = eliminate(small(upper, upper, ((1,), (1,))), upper)
    rows = jnp.where(slot == 0, rows, rows_over(rows))
    basis = rows.T
    if own_slot is not None:
        basis = jnp.where(own_slot == 0, basis, rows_over(basis))
    return basis


def lay_weights(basis, weights_ref, packed):
    low = places()[1] < HALF
    over = lanes_over(basis)
    top = jnp.concatenate([jnp.where(low, basis, 0.0), jnp.where(low, over, 0.0)], axis=1)
    bottom = jnp.concatenate([jnp.where(low, 0.0, over), jnp.where(low, 0.0, basis)], axis=1)
    if packed:
        pieces = [top[:HALF], bottom[:HALF], top[HALF:], bottom[HALF:]]
    else:
        pieces = [top, bottom]
    weights_ref[...] = jnp.concatenate(pieces, axis=0)


def quarters(leaving, cross, staying):
    row, col = places()
    first = jnp.where(col < HALF, leaving, cross)
    second = jnp.where(col < HALF, cross.T, staying)
    return jnp.where(row < HALF, first, second)


def turned(gram, basis):
    return small(basis, small(gram, basis), ((0,), (0,)))


def first_kernel(slots_ref, parts_ref, weights_ref, sums_ref):
    gram = (parts_ref[0] + parts_ref[1]) + (parts_ref[2] + parts_ref[3])
    add_up(gram, sums_ref)
    basis = rotate(gram, None, slots_ref[0, 0])
    lay_weights(basis, weights_ref, False)


def second_kernel(slots_ref, parts_ref, weights_ref, sums_ref, note_ref):
    both = (parts_ref[0] + parts_ref[1]) + (parts_ref[2] + parts_ref[3])
    gram, cross = both[:, :WIDTH], both[:, WIDTH:]
    add_up(gram, sums_ref)
    basis = rotate(gram, slots_ref[0, 0], slots_ref[1, 0])
    note_ref[0] = basis
    note_ref[1] = turned(gram, basis)
    note_ref[2] = cross
    lay_weights(basis, weights_ref, True)


def third_kernel(slots_ref, behind_ref, own_ref, weights_ref, sums_ref, note_ref):
    cross = small(small(behind_ref[0], behind_ref[2], ((0,), (0,))), own_ref[0])
    gram = quarters(behind_ref[1], cross, own_ref[1])
    add_up(gram, sums_ref)
    basis = rotate(gram, slots_ref[1, 0], slots_ref[2, 0])
    note_ref[0] = basis
    note_ref[1] = turned(gram, basis)
    note_ref[2] = cross
    lay_weights(basis, weights_ref, True)


def far_kernel(parts_ref, own_ref, far_ref):
    cross = (parts_ref[0] + parts_ref[1]) + (parts_ref[2] + parts_ref[3])
    far_ref[...] = small(own_ref[0], cross, ((0,), (0,)))


def meet_kernel(old_ref, own_old_ref, behind_ref, own_ref, far_ref, gram_ref, sums_ref):
    row, col = places()
    far = small(far_ref[...], own_old_ref[0])
    first = jnp.where(col < HALF, behind_ref[2], far)
    second = jnp.where(col < HALF, old_ref[1], own_ref[2])
    cross = jnp.where(row < HALF, first, second)
    cross = small(small(behind_ref[0], cross, ((0,), (0,))), own_ref[0])
    gram = quarters(behind_ref[1], cross, own_ref[1])
    gram_ref[...] = gram
    add_up(gram, sums_ref)


def fourth_kernel(slots_ref, gram_ref, weights_ref, norms_ref):
    gram = gram_ref[...]
    basis = rotate(gram, slots_ref[2, 0], slots_ref[3, 0])
    norms_ref[...] = jnp.sum(basis * small(gram, basis), axis=0, keepdims=True)
    lay_weights(basis, weights_ref, True)


WEIGHTS = jax.ShapeDtypeStruct((2 * WIDTH, 2 * WIDTH), F32)
SUMS = jax.ShapeDtypeStruct((2, WIDTH), F32)
NOTE = jax.ShapeDtypeStruct((3, WIDTH, WIDTH), F32)


VMEM = pl.BlockSpec(memory_space=pltpu.VMEM)


CHEAP = pl.CostEstimate(flops=1, bytes_accessed=1, transcendentals=0)
DEAR = pl.CostEstimate(flops=10**10, bytes_accessed=1, transcendentals=0)


def halves_of(value):
    high = value.astype(BF16)
    return high, (value - high.astype(F32)).astype(BF16)


def dot(left, right, dims=((1,), (0,))):
    return lax.dot_general(left, right, (dims, ((), ())), preferred_element_type=F32)


def round_call(kernel, name, outs, *blocks, slots=None, cost=CHEAP):
    first = () if slots is None else (slots,)
    return pl.pallas_call(
        kernel,
        out_shape=outs,
        in_specs=[SMEM] * len(first) + [VMEM] * len(blocks),
        cost_estimate=cost,
        name=name,
    )(*first, *blocks)


ROOM = pltpu.CompilerParams(vmem_limit_bytes=28 << 20)


def apply_kernel(*refs):
    *blocks, weights_ref, leaving_ref, staying_ref = refs
    rows = leaving_ref.shape[0]
    tall = rows // 4
    upper, lower = halves_of(weights_ref[...])
    for start in range(0, rows, tall):
        if len(blocks) == 1:
            pieces = [blocks[0][start : start + tall], blocks[0][rows + start : rows + start + tall]]
        else:
            pieces = [ref[start : start + tall] for ref in blocks]
        block = jnp.concatenate(pieces, axis=1)
        if block.dtype == BF16:
            out = dot(block, upper) + dot(block, lower)
        else:
            high, low = halves_of(block)
            out = dot(high, upper) + (dot(high, lower) + dot(low, upper))
        leaving_ref[start : start + tall] = out[:, :WIDTH]
        staying_ref[start : start + tall] = out[:, WIDTH:]


def apply(first, second, weights, name):
    blocks = (first,) if second is None else (first, second)
    rows = first.shape[0] * len(blocks) // 2
    out = jax.ShapeDtypeStruct((rows, WIDTH), F32)
    return pl.pallas_call(
        apply_kernel,
        in_specs=[VMEM] * (len(blocks) + 1),
        out_specs=(VMEM, VMEM),
        out_shape=(out, out),
        compiler_params=ROOM,
        cost_estimate=CHEAP,
        name=name,
    )(*blocks, weights)


def gram_kernel(*refs):
    *sources, out_ref = refs
    rows = ((0,), (0,))
    high, low = halves_of(jnp.concatenate([ref[...] for ref in sources[:2]], axis=1))
    low_lanes = lax.broadcasted_iota(jnp.int32, (HALF, WIDTH), 1) < HALF
    upper, lower = halves_of(jnp.concatenate([ref[...] for ref in sources[2:]], axis=1))
    total = dot(high, jnp.concatenate([upper, lower], axis=1), rows)
    wide = upper.shape[1]
    total = total[:, :wide] + (total[:, wide:] + dot(low, upper, rows))
    for pair in range(wide // (2 * WIDTH)):
        for i in range(2):
            folds = []
            for j in range(2):
                lane = WIDTH * (2 * pair + j)
                block = total[WIDTH * i : WIDTH * (i + 1), lane : lane + WIDTH]
                folds.append((block[:HALF], block[HALF:]))
            one = folds[0][0] + lanes_over(folds[0][1])
            two = lanes_over(folds[1][0]) + folds[1][1]
            out_ref[HALF * i : HALF * (i + 1), WIDTH * pair : WIDTH * (pair + 1)] = jnp.where(low_lanes, one, two)


def cross_gram(left, right, name):
    return pl.pallas_call(
        gram_kernel,
        in_specs=[VMEM] * (2 + len(right)),
        out_specs=VMEM,
        out_shape=jax.ShapeDtypeStruct((WIDTH, len(right) * HALF), F32),
        compiler_params=ROOM,
        cost_estimate=CHEAP,
        name=name,
    )(*left, *right)


def unpack_kernel(slots_ref, come_ref, stay_ref, out_ref, top_ref, bottom_ref, sems):
    rows = come_ref.shape[0]
    tall = rows // 4
    front = slots_ref[ROUNDS - 1, 0] == 0
    low = lax.broadcasted_iota(jnp.int32, (tall, WIDTH), 1) < HALF
    copies = []
    for step in range(4):
        part = slice(step * tall, (step + 1) * tall)
        come, stay = come_ref[part], stay_ref[part]
        first, second = jnp.where(front, come, stay), jnp.where(front, stay, come)
        top_ref[part] = jnp.where(low, first, lanes_over(second))
        bottom_ref[part] = jnp.where(low, lanes_over(first), second)
        for side, ref in enumerate((top_ref, bottom_ref)):
            place = out_ref.at[pl.ds(side * rows + step * tall, tall)]
            copies.append(pltpu.make_async_copy(ref.at[pl.ds(step * tall, tall)], place, sems.at[side, step]))
            copies[-1].start()
    for copy in copies:
        copy.wait()


def unpack(slots, come, stay):
    rows = come.shape[0]
    return pl.pallas_call(
        unpack_kernel,
        in_specs=[SMEM, VMEM, VMEM],
        out_specs=pl.BlockSpec(memory_space=pl.ANY),
        out_shape=jax.ShapeDtypeStruct((2 * rows, WIDTH), F32),
        scratch_shapes=[
            pltpu.VMEM((rows, WIDTH), F32),
            pltpu.VMEM((rows, WIDTH), F32),
            pltpu.SemaphoreType.DMA((2, 4)),
        ],
        compiler_params=ROOM,
        cost_estimate=CHEAP,
        name="unpack",
    )(slots, come, stay)


def shift(value, steps):
    count = lax.axis_size(PAIR)
    return lax.ppermute(value, PAIR, [(source, (source + steps) % count) for source in range(count)])


def around(value, steps):
    count = lax.axis_size("z")
    if steps >= count:
        return jnp.zeros_like(value)
    return lax.ppermute(value, "z", [(source, (source - steps) % count) for source in range(count)])


def after(value, *others):
    return lax.optimization_barrier((value,) + others)[0]


def on_device(statistic, initial_basis, slots):
    turn = (WEIGHTS, SUMS)
    part = dot(statistic, statistic, ((0,), (0,)))
    weights, sums1 = round_call(first_kernel, "round1", turn, lax.all_gather(part, ROW), slots=slots)
    left, stay = apply(statistic, None, weights, "factor1")
    stay_ahead = shift(stay, -1)
    left_behind = shift(left, 1)
    left_ahead = shift(left, -1)

    part = cross_gram((left_behind, stay), (left_behind, stay, left, stay_ahead), "gram2")
    stay_far = shift(stay_ahead, -1)
    parts = lax.all_gather(part, ROW)
    v_left, v_stay = apply(initial_basis, None, after(weights, parts), "vectors1")
    v_come = shift(v_left, 1)
    turn = turn + (NOTE,)
    parts = after(parts, left_ahead)
    weights, sums2, note2 = round_call(second_kernel, "round2", turn, parts, slots=slots)
    note2_behind = shift(note2, 1)

    part = cross_gram((left_behind, stay), (left_ahead, stay_far), "gram4")
    far = round_call(far_kernel, "far", SMALL, lax.all_gather(part, ROW), note2)
    v_left, v_stay = apply(v_come, v_stay, after(weights, note2_behind, far), "vectors2")
    v_come = shift(v_left, 1)
    far_behind = shift(far, 2)

    weights, sums3, note3 = round_call(third_kernel, "round3", turn, note2_behind, note2, slots=slots)
    note3_behind = shift(note3, 1)
    v_left, v_stay = apply(v_come, v_stay, after(weights, note3_behind, far_behind), "vectors3")
    v_come = shift(v_left, 1)

    gram, sums4 = round_call(
        meet_kernel, "meet4", (SMALL, SUMS), note2_behind, note2, note3_behind, note3, far_behind
    )
    total = jnp.concatenate([sums1, sums2, sums3, sums4], axis=0)
    total = total + around(total, 4)
    norms = jax.ShapeDtypeStruct((1, WIDTH), F32)
    weights, norms = round_call(fourth_kernel, "round4", (WEIGHTS, norms), gram, slots=slots, cost=DEAR)
    come = shift(norms[:, :HALF], 1)
    total = lax.psum(after(total, weights), "y")
    v_left, v_stay = apply(v_come, v_stay, after(weights, total), "vectors4")
    v_come = shift(v_left, 1)

    total = after(total, v_left)
    total = total + around(total, 1)
    total = total + around(total, 2)
    total = lax.psum(after(total, come), "xh")
    total = jnp.sum(total.reshape(ROUNDS, 2, WIDTH), axis=2)
    own = norms[:, HALF:]
    norms = jnp.where(slots[ROUNDS - 1, 0] == 0, jnp.concatenate([come, own], 1), jnp.concatenate([own, come], 1))
    return unpack(slots, v_come, v_stay), jnp.sqrt(norms[0]), jnp.sqrt(total[:, 0] / total[:, 1])


def solution(mesh):
    grid = Mesh(mesh.devices.reshape(2, 8, 8, 2, 2), PAIR + ROW)
    return jax.shard_map(
        on_device,
        mesh=grid,
        in_specs=(P(ROW, PAIR), P(ROW, PAIR), P(None, PAIR)),
        out_specs=(P(ROW, PAIR), P(PAIR), P()),
        check_vma=False,
    )
```

```python
import jax
import jax.numpy as jnp
from jax import lax
from jax.experimental import pallas as pl
from jax.experimental.pallas import tpu as pltpu
from jax.sharding import Mesh
from jax.sharding import PartitionSpec as P

ROUNDS = 4
PAIR = ("xh", "y", "z")
ROW = ("xl", "core")
SUB, WIDTH = 8, 128
TILES = WIDTH // SUB
HALF = WIDTH // 2
F32, BF16 = jnp.float32, jnp.bfloat16
HIGHEST = lax.Precision.HIGHEST
SMALL = jax.ShapeDtypeStruct((WIDTH, WIDTH), F32)
SMEM = pl.BlockSpec(memory_space=pltpu.SMEM)


def spread(value):
    return jnp.broadcast_to(value, (SUB, WIDTH))


def tiles_of(matrix):
    return [matrix[SUB * t : SUB * (t + 1), :] for t in range(TILES)]


def eliminate(square, beside):
    square = tiles_of(square)
    beside = None if beside is None else tiles_of(beside)
    sub = lax.broadcasted_iota(jnp.int32, (SUB, WIDTH), 0)
    lane = lax.broadcasted_iota(jnp.int32, (SUB, WIDTH), 1)
    upper, solved = [], []
    for k in range(TILES):
        left = TILES - k
        cols = [[spread(square[t][:, SUB * k + m : SUB * k + m + 1]) for t in range(k, TILES)] for m in range(SUB)]
        pivots = None
        for j in range(SUB):
            pivot = spread(cols[j][0][j : j + 1, :])
            pivots = pivot if pivots is None else jnp.where(sub >= j, pivot, pivots)
            inverse = 1.0 / pivot
            coef = [c * inverse for c in cols[j]]
            coef[0] = jnp.where(sub > j, coef[0], 0.0)
            for m in range(j + 1, SUB):
                row = spread(cols[m][0][j : j + 1, :])
                for i in range(left):
                    cols[m][i] = cols[m][i] - coef[i] * row
            row = spread(square[k][j : j + 1, :])
            aside = None if beside is None else spread(beside[k][j : j + 1, :])
            for i in range(left):
                if i == 0 and j == SUB - 1:
                    continue
                square[k + i] = square[k + i] - coef[i] * row
                if beside is not None:
                    beside[k + i] = beside[k + i] - coef[i] * aside
        scale = lax.rsqrt(pivots)
        upper.append(jnp.where(lane >= sub + SUB * k, square[k] * scale, 0.0))
        if beside is not None:
            solved.append(beside[k] * scale)
    return jnp.concatenate(upper, axis=0), (jnp.concatenate(solved, axis=0) if solved else None)


def small(left, right, dims=((1,), (0,))):
    return lax.dot_general(left, right, (dims, ((), ())), precision=HIGHEST, preferred_element_type=F32)


def lanes_over(value):
    return pltpu.roll(value, HALF, 1)


def rows_over(value):
    return jnp.concatenate([value[HALF:], value[:HALF]], axis=0)


def places():
    row = lax.broadcasted_iota(jnp.int32, (WIDTH, WIDTH), 0)
    col = lax.broadcasted_iota(jnp.int32, (WIDTH, WIDTH), 1)
    return row, col


def add_up(gram, sums_ref):
    row, col = places()
    squares = gram * gram
    off = jnp.sum(jnp.where(row == col, 0.0, squares), axis=0, keepdims=True)
    diag = jnp.sum(jnp.where(row == col, squares, 0.0), axis=0, keepdims=True)
    sums_ref[...] = jnp.concatenate([off, diag], axis=0)


def rotate(gram, own_slot, slot):
    placed = gram
    if own_slot is not None:
        placed = jnp.where(own_slot == 0, gram, rows_over(lanes_over(gram)))
    upper, _ = eliminate(small(placed, placed, ((0,), (0,))), None)
    _, rows = eliminate(small(upper, upper, ((1,), (1,))), upper)
    rows = jnp.where(slot == 0, rows, rows_over(rows))
    basis = rows.T
    if own_slot is not None:
        basis = jnp.where(own_slot == 0, basis, rows_over(basis))
    return basis


def lay_weights(basis, weights_ref, packed):
    low = places()[1] < HALF
    over = lanes_over(basis)
    top = jnp.concatenate([jnp.where(low, basis, 0.0), jnp.where(low, over, 0.0)], axis=1)
    bottom = jnp.concatenate([jnp.where(low, 0.0, over), jnp.where(low, 0.0, basis)], axis=1)
    if packed:
        pieces = [top[:HALF], bottom[:HALF], top[HALF:], bottom[HALF:]]
    else:
        pieces = [top, bottom]
    weights_ref[...] = jnp.concatenate(pieces, axis=0)


def quarters(leaving, cross, staying):
    row, col = places()
    first = jnp.where(col < HALF, leaving, cross)
    second = jnp.where(col < HALF, cross.T, staying)
    return jnp.where(row < HALF, first, second)


def turned(gram, basis):
    return small(basis, small(gram, basis), ((0,), (0,)))


def first_kernel(slots_ref, parts_ref, weights_ref, sums_ref):
    gram = (parts_ref[0] + parts_ref[1]) + (parts_ref[2] + parts_ref[3])
    add_up(gram, sums_ref)
    basis = rotate(gram, None, slots_ref[0, 0])
    lay_weights(basis, weights_ref, False)


def second_kernel(slots_ref, parts_ref, weights_ref, sums_ref, note_ref):
    both = (parts_ref[0] + parts_ref[1]) + (parts_ref[2] + parts_ref[3])
    gram, cross = both[:, :WIDTH], both[:, WIDTH:]
    add_up(gram, sums_ref)
    basis = rotate(gram, slots_ref[0, 0], slots_ref[1, 0])
    note_ref[0] = basis
    note_ref[1] = turned(gram, basis)
    note_ref[2] = cross
    lay_weights(basis, weights_ref, True)


def third_kernel(slots_ref, behind_ref, own_ref, weights_ref, sums_ref, note_ref):
    cross = small(small(behind_ref[0], behind_ref[2], ((0,), (0,))), own_ref[0])
    gram = quarters(behind_ref[1], cross, own_ref[1])
    add_up(gram, sums_ref)
    basis = rotate(gram, slots_ref[1, 0], slots_ref[2, 0])
    note_ref[0] = basis
    note_ref[1] = turned(gram, basis)
    note_ref[2] = cross
    lay_weights(basis, weights_ref, True)


def far_kernel(parts_ref, own_ref, far_ref):
    cross = (parts_ref[0] + parts_ref[1]) + (parts_ref[2] + parts_ref[3])
    far_ref[...] = small(own_ref[0], cross, ((0,), (0,)))


def meet_kernel(old_ref, own_old_ref, behind_ref, own_ref, far_ref, gram_ref, sums_ref):
    row, col = places()
    far = small(far_ref[...], own_old_ref[0])
    first = jnp.where(col < HALF, behind_ref[2], far)
    second = jnp.where(col < HALF, old_ref[1], own_ref[2])
    cross = jnp.where(row < HALF, first, second)
    cross = small(small(behind_ref[0], cross, ((0,), (0,))), own_ref[0])
    gram = quarters(behind_ref[1], cross, own_ref[1])
    gram_ref[...] = gram
    add_up(gram, sums_ref)


def fourth_kernel(slots_ref, gram_ref, weights_ref, norms_ref):
    gram = gram_ref[...]
    basis = rotate(gram, slots_ref[2, 0], slots_ref[3, 0])
    norms_ref[...] = jnp.sum(basis * small(gram, basis), axis=0, keepdims=True)
    lay_weights(basis, weights_ref, True)


WEIGHTS = jax.ShapeDtypeStruct((2 * WIDTH, 2 * WIDTH), F32)
SUMS = jax.ShapeDtypeStruct((2, WIDTH), F32)
NOTE = jax.ShapeDtypeStruct((3, WIDTH, WIDTH), F32)


VMEM = pl.BlockSpec(memory_space=pltpu.VMEM)


CHEAP = pl.CostEstimate(flops=1, bytes_accessed=1, transcendentals=0)
DEAR = pl.CostEstimate(flops=10**10, bytes_accessed=1, transcendentals=0)


def halves_of(value):
    high = value.astype(BF16)
    return high, (value - high.astype(F32)).astype(BF16)


def dot(left, right, dims=((1,), (0,))):
    return lax.dot_general(left, right, (dims, ((), ())), preferred_element_type=F32)


def round_call(kernel, name, outs, *blocks, slots=None, cost=CHEAP):
    first = () if slots is None else (slots,)
    return pl.pallas_call(
        kernel,
        out_shape=outs,
        in_specs=[SMEM] * len(first) + [VMEM] * len(blocks),
        cost_estimate=cost,
        name=name,
    )(*first, *blocks)


ROOM = pltpu.CompilerParams(vmem_limit_bytes=28 << 20)


def apply_kernel(*refs):
    *blocks, weights_ref, leaving_ref, staying_ref = refs
    rows = leaving_ref.shape[0]
    tall = rows // 4
    upper, lower = halves_of(weights_ref[...])
    for start in range(0, rows, tall):
        if len(blocks) == 1:
            pieces = [blocks[0][start : start + tall], blocks[0][rows + start : rows + start + tall]]
        else:
            pieces = [ref[start : start + tall] for ref in blocks]
        block = jnp.concatenate(pieces, axis=1)
        if block.dtype == BF16:
            out = dot(block, upper) + dot(block, lower)
        else:
            high, low = halves_of(block)
            out = dot(high, upper) + (dot(high, lower) + dot(low, upper))
        leaving_ref[start : start + tall] = out[:, :WIDTH]
        staying_ref[start : start + tall] = out[:, WIDTH:]


def apply(first, second, weights, name):
    blocks = (first,) if second is None else (first, second)
    rows = first.shape[0] * len(blocks) // 2
    out = jax.ShapeDtypeStruct((rows, WIDTH), F32)
    return pl.pallas_call(
        apply_kernel,
        in_specs=[VMEM] * (len(blocks) + 1),
        out_specs=(VMEM, VMEM),
        out_shape=(out, out),
        compiler_params=ROOM,
        cost_estimate=CHEAP,
        name=name,
    )(*blocks, weights)


def gram_kernel(*refs):
    *sources, out_ref = refs
    rows = ((0,), (0,))
    high, low = halves_of(jnp.concatenate([ref[...] for ref in sources[:2]], axis=1))
    low_lanes = lax.broadcasted_iota(jnp.int32, (HALF, WIDTH), 1) < HALF
    upper, lower = halves_of(jnp.concatenate([ref[...] for ref in sources[2:]], axis=1))
    total = dot(high, jnp.concatenate([upper, lower], axis=1), rows)
    wide = upper.shape[1]
    total = total[:, :wide] + (total[:, wide:] + dot(low, upper, rows))
    for pair in range(wide // (2 * WIDTH)):
        for i in range(2):
            folds = []
            for j in range(2):
                lane = WIDTH * (2 * pair + j)
                block = total[WIDTH * i : WIDTH * (i + 1), lane : lane + WIDTH]
                folds.append((block[:HALF], block[HALF:]))
            one = folds[0][0] + lanes_over(folds[0][1])
            two = lanes_over(folds[1][0]) + folds[1][1]
            out_ref[HALF * i : HALF * (i + 1), WIDTH * pair : WIDTH * (pair + 1)] = jnp.where(low_lanes, one, two)


def cross_gram(left, right, name):
    return pl.pallas_call(
        gram_kernel,
        in_specs=[VMEM] * (2 + len(right)),
        out_specs=VMEM,
        out_shape=jax.ShapeDtypeStruct((WIDTH, len(right) * HALF), F32),
        compiler_params=ROOM,
        cost_estimate=CHEAP,
        name=name,
    )(*left, *right)


def unpack_kernel(slots_ref, come_ref, stay_ref, out_ref, top_ref, bottom_ref, sems):
    rows = come_ref.shape[0]
    tall = rows // 4
    front = slots_ref[ROUNDS - 1, 0] == 0
    low = lax.broadcasted_iota(jnp.int32, (tall, WIDTH), 1) < HALF
    copies = []
    for step in range(4):
        part = slice(step * tall, (step + 1) * tall)
        come, stay = come_ref[part], stay_ref[part]
        first, second = jnp.where(front, come, stay), jnp.where(front, stay, come)
        top_ref[part] = jnp.where(low, first, lanes_over(second))
        bottom_ref[part] = jnp.where(low, lanes_over(first), second)
        for side, ref in enumerate((top_ref, bottom_ref)):
            place = out_ref.at[pl.ds(side * rows + step * tall, tall)]
            copies.append(pltpu.make_async_copy(ref.at[pl.ds(step * tall, tall)], place, sems.at[side, step]))
            copies[-1].start()
    for copy in copies:
        copy.wait()


def unpack(slots, come, stay):
    rows = come.shape[0]
    return pl.pallas_call(
        unpack_kernel,
        in_specs=[SMEM, VMEM, VMEM],
        out_specs=pl.BlockSpec(memory_space=pl.ANY),
        out_shape=jax.ShapeDtypeStruct((2 * rows, WIDTH), F32),
        scratch_shapes=[
            pltpu.VMEM((rows, WIDTH), F32),
            pltpu.VMEM((rows, WIDTH), F32),
            pltpu.SemaphoreType.DMA((2, 4)),
        ],
        compiler_params=ROOM,
        cost_estimate=CHEAP,
        name="unpack",
    )(slots, come, stay)


def shift(value, steps):
    count = lax.axis_size(PAIR)
    return lax.ppermute(value, PAIR, [(source, (source + steps) % count) for source in range(count)])


def around(value, steps):
    count = lax.axis_size("z")
    if steps >= count:
        return jnp.zeros_like(value)
    return lax.ppermute(value, "z", [(source, (source - steps) % count) for source in range(count)])


def after(value, *others):
    return lax.optimization_barrier((value,) + others)[0]


def on_device(statistic, initial_basis, slots):
    turn = (WEIGHTS, SUMS)
    part = dot(statistic, statistic, ((0,), (0,)))
    weights, sums1 = round_call(first_kernel, "round1", turn, lax.all_gather(part, ROW), slots=slots)
    left, stay = apply(statistic, None, weights, "factor1")
    stay_ahead = shift(stay, -1)
    left_behind = shift(left, 1)

    part = cross_gram((left_behind, stay), (left_behind, stay, left, stay_ahead), "gram2")
    parts = lax.all_gather(part, ROW)
    turn = turn + (NOTE,)
    weights2, sums2, note2 = round_call(second_kernel, "round2", turn, parts, slots=slots)
    note2_behind = shift(note2, 1)
    v_left, v_stay = apply(initial_basis, None, after(weights, note2), "vectors1")
    v_come = shift(v_left, 1)
    left_ahead = shift(after(left, note2), -1)
    stay_far = shift(after(stay_ahead, note2), -1)

    weights3, sums3, note3 = round_call(third_kernel, "round3", turn, note2_behind, note2, slots=slots, cost=DEAR)
    note3_behind = shift(note3, 1)
    v_left, v_stay = apply(v_come, v_stay, after(weights2, note3), "vectors2")
    v_come = shift(v_left, 1)

    part = cross_gram((left_behind, stay), (left_ahead, after(stay_far, note3)), "gram4")
    far = round_call(far_kernel, "far", SMALL, lax.all_gather(part, ROW), note2)
    far_behind = shift(far, 2)
    v_left, v_stay = apply(v_come, v_stay, after(weights3, note3_behind, far), "vectors3")
    v_come = shift(v_left, 1)

    gram, sums4 = round_call(
        meet_kernel, "meet4", (SMALL, SUMS), note2_behind, note2, note3_behind, note3, after(far_behind, v_left)
    )
    total = jnp.concatenate([sums1, sums2, sums3, sums4], axis=0)
    total = total + around(total, 4)
    norms = jax.ShapeDtypeStruct((1, WIDTH), F32)
    weights, norms = round_call(fourth_kernel, "round4", (WEIGHTS, norms), gram, slots=slots, cost=DEAR)
    come = shift(norms[:, :HALF], 1)
    total = lax.psum(after(total, weights), "y")
    v_left, v_stay = apply(v_come, v_stay, after(weights, total, come), "vectors4")
    v_come = shift(v_left, 1)

    total = after(total, v_left)
    total = total + around(total, 1)
    total = total + around(total, 2)
    total = lax.psum(total, "xh")
    total = jnp.sum(total.reshape(ROUNDS, 2, WIDTH), axis=2)
    own = norms[:, HALF:]
    norms = jnp.where(slots[ROUNDS - 1, 0] == 0, jnp.concatenate([come, own], 1), jnp.concatenate([own, come], 1))
    return unpack(slots, v_come, v_stay), jnp.sqrt(norms[0]), jnp.sqrt(total[:, 0] / total[:, 1])


def solution(mesh):
    grid = Mesh(mesh.devices.reshape(2, 8, 8, 2, 2), PAIR + ROW)
    return jax.shard_map(
        on_device,
        mesh=grid,
        in_specs=(P(ROW, PAIR), P(ROW, PAIR), P(None, PAIR)),
        out_specs=(P(ROW, PAIR), P(PAIR), P()),
        check_vma=False,
    )
```
